32 devices in a mesh: src: 4 (over y, x), win: 8 (over z, core).
Axes of the slice: x: 2, y: 2, z: 4, core: 2. Of those that a mesh axis runs over, the one named last changes fastest.
Arguments:
- raw: float32 [64, 262144], P('src', 'win'), may hold values from -800 to 800
- shift: int32 [64], P('src'), may hold values from 3 to 4092, as said below
- frac_bin: int32 [64], P('src'), may hold values from 0 to 63
Outputs:
- stack: float32 [2, 64, 64, 4096], P(None, 'src', None, 'win')
The draws below stay inside these ranges and needn't reach their ends.
Inputs may be any that keep to these rules, and one draw needn't show every extreme that they name: Every node group (nodes g * 16 to g * 16 + 15) holds a node with shift exactly 4092.
All inputs are finite; a program needn't handle non-finite values.
Results may differ from the reference program's by a relative error of at most 0.0039.
Values may be sent and summed in bfloat16 or wider, within the bound.
A program may use at most 64 MiB of HBM per device.

```python
import math
import jax
import jax.numpy as jnp
from jax import lax

F = 4096
BAND = 128
MAXS = 4092
BINS = 64
NPD = 16
NODES = 64
WINDOWS = 32
SAMPLES = 262144
N_WIN = 8


def draw_raw(key, part):
    keys = jax.random.split(key, 5)
    length = 2 * F
    times = jnp.arange(SAMPLES, dtype=jnp.int32) % length
    noise = jnp.clip(jax.random.normal(keys[0], (NODES, SAMPLES), jnp.float32), -5.0, 5.0)
    scales = jnp.exp(jax.random.uniform(keys[1], (NODES,), jnp.float32) * math.log(10.0))
    tone_bins = jax.random.randint(keys[2], (NODES, 4), 1, F)
    amplitudes = jnp.exp(jax.random.uniform(keys[3], (NODES, 4), jnp.float32, math.log(0.3), math.log(8.0)))
    phases = jax.random.uniform(keys[4], (NODES, 4), jnp.float32, -math.pi, math.pi)
    signal = noise
    for tone in range(4):
        cycles = times[None, :] * tone_bins[:, tone:tone + 1] % length
        angle = 2.0 * math.pi * cycles.astype(jnp.float32) / length + phases[:, tone:tone + 1]
        signal = signal + amplitudes[:, tone:tone + 1] * jnp.cos(angle)
    return scales[:, None] * signal


def draw_shift(key, part):
    base_key = jax.random.fold_in(key, 11)
    chosen_key = jax.random.fold_in(key, 12)
    shifts = jax.random.randint(base_key, (NODES,), 3, MAXS + 1)
    groups = NODES // NPD
    chosen = jax.random.randint(chosen_key, (groups,), 0, NPD)
    positions = jnp.arange(groups, dtype=jnp.int32) * NPD + chosen
    return shifts.at[positions].set(MAXS)


def touch_ends(values, own_key, least, top_value):
    dims = values.shape
    place = [jax.random.randint(jax.random.fold_in(own_key, axis), (), 0, dims[axis]) for axis in range(len(dims))]
    values = values.at[tuple(place)].set(least)
    longest = dims.index(max(dims))
    place[longest] = (place[longest] + 1) % dims[longest]
    return values.at[tuple(place)].set(top_value)


def setup_inputs(seed: int = 0) -> dict:
    key_list = jax.random.split(jax.random.key(seed), 4)
    return {
        "raw": draw_raw(jax.random.fold_in(key_list[3], 71), 0),
        "shift": draw_shift(jax.random.fold_in(key_list[3], 71), 0),
        "frac_bin": touch_ends(jax.random.randint(key_list[2], (NODES,), 0, BINS), jax.random.fold_in(key_list[2], 1), 0, BINS - 1).astype(jnp.int32),
    }


def tap_weights(frac_bin):
    offsets = jnp.arange(8, dtype=jnp.float32)
    spacing = offsets[None, :] - 3.0 - frac_bin.astype(jnp.float32)[:, None] / BINS
    return jnp.sinc(spacing) * jnp.sinc(spacing / 4.0)

def resample_rows(extended, shift, weights, length):

    def single_row(samples, offset, taps):
        summed = jnp.zeros((length,), samples.dtype)
        for position in range(8):
            summed = summed + taps[position] * lax.dynamic_slice_in_dim(samples, offset + (position - 3), length)
        return summed
    return jax.vmap(single_row)(extended, shift, weights)

def hann_window(length):
    position = jnp.arange(length, dtype=jnp.float32)
    return 0.5 - 0.5 * jnp.cos(2.0 * jnp.pi * position / length)

def whiten(real_part, imag_part):
    shape = real_part.shape
    bands = shape[-1] // BAND
    real_bands = real_part.reshape(shape[:-1] + (bands, BAND))
    imag_bands = imag_part.reshape(shape[:-1] + (bands, BAND))
    power = lax.optimization_barrier(jnp.mean(real_bands * real_bands + imag_bands * imag_bands, axis=-1))
    denominator = jnp.sqrt(power + 1e-06)[..., None]
    return ((real_bands / denominator).reshape(shape), (imag_bands / denominator).reshape(shape))

def cross_spectra(mine_re, mine_im, other_re, other_im, count):
    real_sum = jnp.einsum('iwf,jwf->ijf', mine_re, other_re) + jnp.einsum('iwf,jwf->ijf', mine_im, other_im)
    imag_sum = jnp.einsum('iwf,jwf->ijf', mine_im, other_re) - jnp.einsum('iwf,jwf->ijf', mine_re, other_im)
    return jnp.stack([real_sum, imag_sum]) / count

def reference(raw, shift, frac_bin):
    extended = jnp.concatenate([raw, jnp.zeros((NODES, MAXS + 4), jnp.float32)], axis=1)
    resampled = resample_rows(extended, shift, tap_weights(frac_bin), SAMPLES)
    segments = resampled.reshape(NODES, WINDOWS, 2 * F) * hann_window(2 * F)
    spectrum = jnp.fft.rfft(segments, axis=-1)[..., :F]
    real_part = jnp.real(spectrum).astype(jnp.float32)
    imag_part = jnp.imag(spectrum).astype(jnp.float32)
    white_re, white_im = whiten(real_part, imag_part)
    white_re = white_re.astype(jnp.bfloat16)
    white_im = white_im.astype(jnp.bfloat16)
    local_freq = F // N_WIN
    re_blocks = white_re.reshape(NODES, WINDOWS, N_WIN, local_freq).transpose(2, 0, 1, 3)
    im_blocks = white_im.reshape(NODES, WINDOWS, N_WIN, local_freq).transpose(2, 0, 1, 3)

    def stack_block(pair):
        block_re = pair[0].astype(jnp.float32)
        block_im = pair[1].astype(jnp.float32)
        return cross_spectra(block_re, block_im, block_re, block_im, WINDOWS)
    stacked = lax.map(stack_block, (re_blocks, im_blocks))
    return stacked.transpose(1, 2, 3, 0, 4).reshape(2, NODES, NODES, F)
```

```python
import functools

import jax
import jax.numpy as jnp
import ml_dtypes
import numpy as np
from jax import lax
from jax.experimental import pallas as pl
from jax.experimental.pallas import tpu as pltpu
from jax.sharding import PartitionSpec as P

F = 4096
BAND = 128
MAXS = 4092
BINS = 64
LANES = 128
ROWS = 2 * F // LANES
BANDS = F // BAND
HEAD = (MAXS + 4) // LANES
VMEM_LIMIT = 48 * 1024 * 1024


def tap_weights(frac_bin):
    offsets = jnp.arange(8, dtype=jnp.float32)
    spacing = offsets[None, :] - 3.0 - frac_bin.astype(jnp.float32)[:, None] / BINS
    return jnp.sinc(spacing) * jnp.sinc(spacing / 4.0)


def split_columns(matrix):
    high = matrix.astype(ml_dtypes.bfloat16)
    low = (matrix - high.astype(np.float64)).astype(ml_dtypes.bfloat16)
    return np.concatenate([high, high, low], axis=1)


def tables():
    r = np.arange(ROWS)
    lane = np.arange(LANES)
    band = np.arange(BANDS)
    first = 2 * np.pi * (np.outer(r, r) % ROWS) / ROWS
    first = split_columns(np.concatenate([np.cos(first), -np.sin(first)], axis=0))
    turn = 2 * np.pi * (np.outer(lane, lane) % (2 * F)) / (2 * F)
    twist = np.stack([np.cos(turn), np.sin(turn)]).astype(np.float32)
    second = 2 * np.pi * (np.outer(band, lane) % ROWS) / ROWS
    cos, sin = np.cos(second), np.sin(second)
    second = split_columns(np.block([[cos, sin], [-sin, cos]]))
    position = np.arange(2 * F).reshape(ROWS, LANES)
    hann = (0.5 - 0.5 * np.cos(2 * np.pi * position / (2 * F))).astype(np.float32)
    return first, twist, second, hann


def split_value(value):
    high = value.astype(jnp.bfloat16)
    low = (value - high.astype(jnp.float32)).astype(jnp.bfloat16)
    return high, low


def spectra_kernel(
    windows, shift_ref, taps_ref, raw_ref, next_ref, first_ref, twist_ref, second_ref, hann_ref,
    out_ref, line, white,
):
    node = pl.program_id(0)
    nodes = pl.num_programs(0)
    length = windows * ROWS
    line[0:length, :] = raw_ref[0]
    line[length : length + HEAD, :] = next_ref[0].astype(jnp.float32)
    line[length + HEAD : length + HEAD + 8, :] = jnp.zeros((8, LANES), jnp.float32)
    lane = lax.broadcasted_iota(jnp.int32, (ROWS, LANES), 1)
    columns = []
    for w in range(windows):
        total = jnp.zeros((ROWS, LANES), jnp.float32)
        for tap in range(8):
            offset = shift_ref[node] + (tap - 3)
            row, by = offset // LANES, offset % LANES
            here = line[pl.ds(row + w * ROWS, ROWS), :]
            after = line[pl.ds(row + w * ROWS + 1, ROWS), :]
            joined = jnp.where(lane >= by, here, after)
            total = total + taps_ref[node, tap] * pltpu.roll(joined, (LANES - by) % LANES, 1)
        high, low = split_value(total * hann_ref[...])
        columns.append(jnp.concatenate([high, low, high], axis=0))
    section = jnp.dot(
        first_ref[...], jnp.concatenate(columns, axis=1), preferred_element_type=jnp.float32
    )
    turned = []
    for w in range(windows):
        re = section[:ROWS, w * LANES : (w + 1) * LANES]
        im = section[ROWS:, w * LANES : (w + 1) * LANES]
        for half in range(2):
            cos = twist_ref[0, half * ROWS : (half + 1) * ROWS, :]
            sin = twist_ref[1, half * ROWS : (half + 1) * ROWS, :]
            re_high, re_low = split_value(re * cos + im * sin)
            im_high, im_low = split_value(im * cos - re * sin)
            turned.append(
                jnp.concatenate([re_high, im_high, re_low, im_low, re_high, im_high], axis=1)
            )
    final = lax.dot_general(
        second_ref[...],
        jnp.concatenate(turned, axis=0),
        (((1,), (1,)), ((), ())),
        preferred_element_type=jnp.float32,
    )
    count = out_ref.shape[4]
    for w in range(windows):
        re = final[:BANDS, w * LANES : (w + 1) * LANES]
        im = final[BANDS:, w * LANES : (w + 1) * LANES]
        power = jnp.sum(re * re + im * im, axis=-1, keepdims=True) / BAND
        scale = lax.rsqrt(power + 1e-06)
        for part, value in ((0, re), (1, im)):
            start = (part * windows + w) * BANDS * count + node
            white[pl.ds(start, BANDS, stride=count), :] = value * scale

    @pl.when(node == nodes - 1)
    def _():
        owners, owned = out_ref.shape[0], out_ref.shape[3]
        for part in range(2):
            for w in range(windows):
                start = (part * windows + w) * BANDS * count
                block = white[start : start + BANDS * count, :].astype(jnp.bfloat16)
                out_ref[:, part, w] = block.reshape(owners, owned, count, LANES)


def spectra(raw, following, shift, taps, owners):
    nodes, rows = raw.shape[:2]
    windows = rows // ROWS
    owned = BANDS // owners
    first, twist, second, hann = tables()
    shape = (owners, 2, windows, owned, nodes, LANES)
    whole = lambda array: pl.BlockSpec(array.shape, lambda i: (0,) * array.ndim)
    return pl.pallas_call(
        functools.partial(spectra_kernel, windows),
        grid=(nodes,),
        out_shape=jax.ShapeDtypeStruct(shape, jnp.bfloat16),
        in_specs=[
            pl.BlockSpec(memory_space=pltpu.SMEM),
            pl.BlockSpec(memory_space=pltpu.SMEM),
            pl.BlockSpec((1, rows, LANES), lambda i: (i, 0, 0)),
            pl.BlockSpec((1, HEAD, LANES), lambda i: (i, 0, 0)),
            whole(first),
            whole(twist),
            whole(second),
            whole(hann),
        ],
        out_specs=pl.BlockSpec(shape, lambda i: (0,) * 6),
        scratch_shapes=[
            pltpu.VMEM((rows + HEAD + 8, LANES), jnp.float32),
            pltpu.VMEM((2 * windows * BANDS * nodes, LANES), jnp.float32),
        ],
        compiler_params=pltpu.CompilerParams(vmem_limit_bytes=VMEM_LIMIT),
    )(shift, taps, raw, following, jnp.asarray(first), jnp.asarray(twist), jnp.asarray(second), jnp.asarray(hann))


def cross_group(held, read_other, write, owners, windows, owned, nodes):
    scale = 1.0 / (owners * windows)
    step = 8

    for band in range(owned):
        for chunk in range(nodes // step):

            def body(owner, sums):
                sums = list(sums)
                for w in range(windows):
                    other_re = read_other(owner, 0, w, band).astype(jnp.float32)
                    other_im = read_other(owner, 1, w, band).astype(jnp.float32)
                    other_diff = other_re - other_im
                    for k in range(step):
                        i = chunk * step + k
                        base = 3 * k
                        sums[base] += held[0, owner, w, band, i : i + 1, :] * other_re
                        sums[base + 1] += held[1, owner, w, band, i : i + 1, :] * other_im
                        sums[base + 2] += held[2, owner, w, band, i : i + 1, :] * other_diff
                return tuple(sums)

            zero = jnp.zeros((nodes, LANES), jnp.float32)
            sums = lax.fori_loop(0, owners, body, (zero,) * (3 * step))
            for k in range(step):
                p, q, r = sums[3 * k : 3 * k + 3]
                write(0, chunk * step + k, band, (p + q) * scale)
                write(1, chunk * step + k, band, (r - p + q) * scale)


def hold(held, read_own, owners, windows):

    def body(owner, carry):
        for w in range(windows):
            re = read_own(owner, 0, w).astype(jnp.float32)
            im = read_own(owner, 1, w).astype(jnp.float32)
            held[0, owner, w] = re
            held[1, owner, w] = im
            held[2, owner, w] = re + im
        return carry

    lax.fori_loop(0, owners, body, 0)


def cross_kernel(own_ref, all_ref, out_ref, held):
    owners, _, windows, owned, nodes, _ = own_ref.shape

    @pl.when(pl.program_id(0) == 0)
    def _():
        hold(held, lambda o, c, w: own_ref[o, c, w], owners, windows)

    def write(part, i, band, value):
        out_ref[part, i, :, band * LANES : (band + 1) * LANES] = value

    cross_group(
        held, lambda o, c, w, b: all_ref[0, o, c, w, b], write, owners, windows, owned, nodes
    )


def cross(own, everyone):
    owners, _, windows, owned, nodes, _ = own.shape
    groups = everyone.shape[0]
    return pl.pallas_call(
        cross_kernel,
        grid=(groups,),
        out_shape=jax.ShapeDtypeStruct((2, nodes, groups * nodes, owned * LANES), jnp.float32),
        in_specs=[
            pl.BlockSpec(own.shape, lambda g: (0,) * 6),
            pl.BlockSpec((1,) + own.shape, lambda g: (g, 0, 0, 0, 0, 0, 0)),
        ],
        out_specs=pl.BlockSpec((2, nodes, nodes, owned * LANES), lambda g: (0, 0, g, 0)),
        scratch_shapes=[pltpu.VMEM((3, owners, windows, owned, nodes, LANES), jnp.float32)],
        compiler_params=pltpu.CompilerParams(vmem_limit_bytes=VMEM_LIMIT),
    )(own, everyone)


def local(raw, shift, frac_bin):
    owners = lax.axis_size("win")
    raw = raw.reshape(raw.shape[0], -1, LANES)
    heading = raw[:, :HEAD].astype(jnp.bfloat16)
    following = lax.ppermute(heading, "win", [(i, i - 1) for i in range(1, owners)])
    white = spectra(raw, following, shift, tap_weights(frac_bin), owners)
    own = lax.all_to_all(white, "win", split_axis=0, concat_axis=0, tiled=True)
    everyone = lax.all_gather(own, "src", axis=0)
    return cross(own, everyone)


def solution(mesh):
    return jax.shard_map(
        local,
        mesh=mesh,
        in_specs=(P("src", "win"), P("src"), P("src")),
        out_specs=P(None, "src", None, "win"),
        check_vma=False,
    )
```

```python
import functools

import jax
import jax.numpy as jnp
import ml_dtypes
import numpy as np
from jax import lax
from jax.experimental import pallas as pl
from jax.experimental.pallas import tpu as pltpu
from jax.sharding import PartitionSpec as P

F = 4096
BAND = 128
MAXS = 4092
BINS = 64
LANES = 128
ROWS = 2 * F // LANES
BANDS = F // BAND
HEAD = (MAXS + 4) // LANES
VMEM_LIMIT = 48 * 1024 * 1024
MESH = pl.DeviceIdType.MESH


def tap_weights(frac_bin):
    offsets = jnp.arange(8, dtype=jnp.float32)
    spacing = offsets[None, :] - 3.0 - frac_bin.astype(jnp.float32)[:, None] / BINS
    return jnp.sinc(spacing) * jnp.sinc(spacing / 4.0)


def split_columns(matrix):
    high = matrix.astype(ml_dtypes.bfloat16)
    low = (matrix - high.astype(np.float64)).astype(ml_dtypes.bfloat16)
    return np.concatenate([high, high, low], axis=1)


def tables():
    r = np.arange(ROWS)
    lane = np.arange(LANES)
    band = np.arange(BANDS)
    first = 2 * np.pi * (np.outer(r, r) % ROWS) / ROWS
    first = split_columns(np.concatenate([np.cos(first), -np.sin(first)], axis=0))
    turn = 2 * np.pi * (np.outer(lane, lane) % (2 * F)) / (2 * F)
    twist = np.stack([np.cos(turn), np.sin(turn)]).astype(np.float32)
    second = 2 * np.pi * (np.outer(band, lane) % ROWS) / ROWS
    cos, sin = np.cos(second), np.sin(second)
    second = split_columns(np.block([[cos, sin], [-sin, cos]]))
    position = np.arange(2 * F).reshape(ROWS, LANES)
    hann = (0.5 - 0.5 * np.cos(2 * np.pi * position / (2 * F))).astype(np.float32)
    return first, twist, second, hann


def split_value(value):
    high = value.astype(jnp.bfloat16)
    low = (value - high.astype(jnp.float32)).astype(jnp.bfloat16)
    return high, low


def spectra_kernel(
    windows, shift_ref, taps_ref, raw_ref, next_ref, first_ref, twist_ref, second_ref, hann_ref,
    out_ref, line, white,
):
    node = pl.program_id(0)
    nodes = pl.num_programs(0)
    length = windows * ROWS
    line[0:length, :] = raw_ref[0]
    line[length : length + HEAD, :] = next_ref[0].astype(jnp.float32)
    line[length + HEAD : length + HEAD + 8, :] = jnp.zeros((8, LANES), jnp.float32)
    lane = lax.broadcasted_iota(jnp.int32, (ROWS, LANES), 1)
    columns = []
    for w in range(windows):
        total = jnp.zeros((ROWS, LANES), jnp.float32)
        for tap in range(8):
            offset = shift_ref[node] + (tap - 3)
            row, by = offset // LANES, offset % LANES
            here = line[pl.ds(row + w * ROWS, ROWS), :]
            after = line[pl.ds(row + w * ROWS + 1, ROWS), :]
            joined = jnp.where(lane >= by, here, after)
            total = total + taps_ref[node, tap] * pltpu.roll(joined, (LANES - by) % LANES, 1)
        high, low = split_value(total * hann_ref[...])
        columns.append(jnp.concatenate([high, low, high], axis=0))
    section = jnp.dot(
        first_ref[...], jnp.concatenate(columns, axis=1), preferred_element_type=jnp.float32
    )
    turned = []
    for w in range(windows):
        re = section[:ROWS, w * LANES : (w + 1) * LANES]
        im = section[ROWS:, w * LANES : (w + 1) * LANES]
        for half in range(2):
            cos = twist_ref[0, half * ROWS : (half + 1) * ROWS, :]
            sin = twist_ref[1, half * ROWS : (half + 1) * ROWS, :]
            re_high, re_low = split_value(re * cos + im * sin)
            im_high, im_low = split_value(im * cos - re * sin)
            turned.append(
                jnp.concatenate([re_high, im_high, re_low, im_low, re_high, im_high], axis=1)
            )
    final = lax.dot_general(
        second_ref[...],
        jnp.concatenate(turned, axis=0),
        (((1,), (1,)), ((), ())),
        preferred_element_type=jnp.float32,
    )
    count = out_ref.shape[4]
    for w in range(windows):
        re = final[:BANDS, w * LANES : (w + 1) * LANES]
        im = final[BANDS:, w * LANES : (w + 1) * LANES]
        power = jnp.sum(re * re + im * im, axis=-1, keepdims=True) / BAND
        scale = lax.rsqrt(power + 1e-06)
        for part, value in ((0, re), (1, im)):
            start = (part * windows + w) * BANDS * count + node
            white[pl.ds(start, BANDS, stride=count), :] = value * scale

    @pl.when(node == nodes - 1)
    def _():
        owners, owned = out_ref.shape[0], out_ref.shape[3]
        for part in range(2):
            for w in range(windows):
                start = (part * windows + w) * BANDS * count
                block = white[start : start + BANDS * count, :].astype(jnp.bfloat16)
                out_ref[:, part, w] = block.reshape(owners, owned, count, LANES)


def spectra(raw, following, shift, taps, owners):
    nodes, rows = raw.shape[:2]
    windows = rows // ROWS
    owned = BANDS // owners
    first, twist, second, hann = tables()
    shape = (owners, 2, windows, owned, nodes, LANES)
    whole = lambda array: pl.BlockSpec(array.shape, lambda i: (0,) * array.ndim)
    return pl.pallas_call(
        functools.partial(spectra_kernel, windows),
        grid=(nodes,),
        out_shape=jax.ShapeDtypeStruct(shape, jnp.bfloat16),
        in_specs=[
            pl.BlockSpec(memory_space=pltpu.SMEM),
            pl.BlockSpec(memory_space=pltpu.SMEM),
            pl.BlockSpec((1, rows, LANES), lambda i: (i, 0, 0)),
            pl.BlockSpec((1, HEAD, LANES), lambda i: (i, 0, 0)),
            whole(first),
            whole(twist),
            whole(second),
            whole(hann),
        ],
        out_specs=pl.BlockSpec(shape, lambda i: (0,) * 6),
        scratch_shapes=[
            pltpu.VMEM((rows + HEAD + 8, LANES), jnp.float32),
            pltpu.VMEM((2 * windows * BANDS * nodes, LANES), jnp.float32),
        ],
        compiler_params=pltpu.CompilerParams(vmem_limit_bytes=VMEM_LIMIT),
    )(shift, taps, raw, following, jnp.asarray(first), jnp.asarray(twist), jnp.asarray(second), jnp.asarray(hann))


def exchange_kernel(
    lag, white_ref, out_ref, recv, held, send_sem, recv_sem, out_sem, in_sem, own_sem
):
    owners, _, windows, owned, nodes, _ = white_ref.shape
    groups = recv.shape[0]
    scale = 1.0 / (owners * windows)
    step = 8
    me_w, me_g = lax.axis_index("win"), lax.axis_index("src")

    def wrap(index, count):
        return lax.rem(index + count, count)

    barrier = pltpu.get_barrier_semaphore()
    for d in range(1, owners):
        pl.semaphore_signal(
            barrier, inc=1, device_id={"win": wrap(me_w + d, owners)}, device_id_type=MESH
        )
    for e in range(1, groups):
        pl.semaphore_signal(
            barrier, inc=1, device_id={"src": wrap(me_g + e, groups)}, device_id_type=MESH
        )
    own = pltpu.make_async_copy(white_ref.at[me_w], recv.at[me_g, me_w], own_sem)
    own.start()
    out_ref[...] = jnp.zeros_like(out_ref)
    pl.semaphore_wait(barrier, owners + groups - 2)

    def across(d):
        target = wrap(me_w + d, owners)
        return pltpu.make_async_remote_copy(
            src_ref=white_ref.at[target],
            dst_ref=recv.at[me_g, me_w],
            send_sem=send_sem.at[d],
            recv_sem=recv_sem.at[d],
            device_id={"win": target},
            device_id_type=MESH,
        )

    def arriving(d):
        return pltpu.make_async_remote_copy(
            src_ref=white_ref.at[me_w],
            dst_ref=recv.at[me_g, wrap(me_w - d, owners)],
            send_sem=send_sem.at[d],
            recv_sem=recv_sem.at[d],
            device_id={"win": wrap(me_w + d, owners)},
            device_id_type=MESH,
        )

    def forward(e, d):
        slot = wrap(me_w - d, owners)
        return pltpu.make_async_remote_copy(
            src_ref=recv.at[me_g, slot],
            dst_ref=recv.at[me_g, slot],
            send_sem=out_sem.at[e, d],
            recv_sem=in_sem.at[e, d],
            device_id={"src": wrap(me_g + e, groups)},
            device_id_type=MESH,
        )

    def forwarded(e, d):
        slot = wrap(me_w - d, owners)
        group = wrap(me_g - e, groups)
        return pltpu.make_async_remote_copy(
            src_ref=recv.at[group, slot],
            dst_ref=recv.at[group, slot],
            send_sem=out_sem.at[e, d],
            recv_sem=in_sem.at[e, d],
            device_id={"src": wrap(me_g + e, groups)},
            device_id_type=MESH,
        )

    def hold(slot):
        for w in range(windows):
            re = recv[me_g, slot, 0, w].astype(jnp.float32) * scale
            im = recv[me_g, slot, 1, w].astype(jnp.float32) * scale
            held[0, slot, w] = re
            held[1, slot, w] = im
            held[2, slot, w] = re + im

    def add(group, slot):
        rows = pl.ds(pl.multiple_of(group * nodes, nodes), nodes)

        def body(band, carry):
            columns = pl.ds(pl.multiple_of(band * LANES, LANES), LANES)
            for chunk in range(nodes // step):
                sums = [jnp.zeros((nodes, LANES), jnp.float32)] * (3 * step)
                for w in range(windows):
                    other_re = recv[group, slot, 0, w, band].astype(jnp.float32)
                    other_im = recv[group, slot, 1, w, band].astype(jnp.float32)
                    other_diff = other_re - other_im
                    for k in range(step):
                        i = chunk * step + k
                        sums[3 * k] += held[0, slot, w, band, i : i + 1, :] * other_re
                        sums[3 * k + 1] += held[1, slot, w, band, i : i + 1, :] * other_im
                        sums[3 * k + 2] += held[2, slot, w, band, i : i + 1, :] * other_diff
                for k in range(step):
                    p, q, r = sums[3 * k : 3 * k + 3]
                    i = chunk * step + k
                    out_ref[0, i, rows, columns] += p + q
                    out_ref[1, i, rows, columns] += r - p + q
            return carry

        lax.fori_loop(0, owned, body, 0)

    def send(d, carry):
        across(d).start()
        return carry

    lax.fori_loop(1, owners, send, 0)
    own.wait()

    def arrive(d):
        for e in range(1, groups):
            forward(e, d).start()
        slot = wrap(me_w - d, owners)
        hold(slot)
        add(me_g, slot)

    def finish(d):
        slot = wrap(me_w - d, owners)

        def body(e, carry):
            forwarded(e, d).wait_recv()
            add(wrap(me_g - e, groups), slot)
            return carry

        lax.fori_loop(1, groups, body, 0)

    def first(d, carry):
        arriving(d).wait_recv()
        arrive(d)
        return carry

    def middle(d, carry):
        arriving(d).wait_recv()
        arrive(d)
        finish(d - lag)
        return carry

    def last(d, carry):
        finish(d)
        return carry

    arrive(0)
    lax.fori_loop(1, lag, first, 0)
    lax.fori_loop(lag, owners, middle, 0)
    lax.fori_loop(owners - lag, owners, last, 0)

    def sent(d, carry):
        across(d).wait_send()
        return carry

    lax.fori_loop(1, owners, sent, 0)

    def passed(d, carry):
        for e in range(1, groups):
            forward(e, d).wait_send()
        return carry

    lax.fori_loop(0, owners, passed, 0)


def exchange(white, groups):
    owners, _, windows, owned, nodes, _ = white.shape
    return pl.pallas_call(
        functools.partial(exchange_kernel, min(2, owners - 1)),
        out_shape=jax.ShapeDtypeStruct((2, nodes, groups * nodes, owned * LANES), jnp.float32),
        in_specs=[pl.BlockSpec(memory_space=pltpu.VMEM)],
        out_specs=pl.BlockSpec(memory_space=pltpu.VMEM),
        scratch_shapes=[
            pltpu.VMEM((groups,) + white.shape, jnp.bfloat16),
            pltpu.VMEM((3, owners, windows, owned, nodes, LANES), jnp.float32),
            pltpu.SemaphoreType.DMA((owners,)),
            pltpu.SemaphoreType.DMA((owners,)),
            pltpu.SemaphoreType.DMA((groups, owners)),
            pltpu.SemaphoreType.DMA((groups, owners)),
            pltpu.SemaphoreType.DMA,
        ],
        compiler_params=pltpu.CompilerParams(
            collective_id=0, has_side_effects=True, vmem_limit_bytes=VMEM_LIMIT
        ),
    )(white)


def local(raw, shift, frac_bin):
    owners = lax.axis_size("win")
    raw = raw.reshape(raw.shape[0], -1, LANES)
    heading = raw[:, :HEAD].astype(jnp.bfloat16)
    following = lax.ppermute(heading, "win", [(i, i - 1) for i in range(1, owners)])
    white = spectra(raw, following, shift, tap_weights(frac_bin), owners)
    return exchange(white, lax.axis_size("src"))


def solution(mesh):
    return jax.shard_map(
        local,
        mesh=mesh,
        in_specs=(P("src", "win"), P("src"), P("src")),
        out_specs=P(None, "src", None, "win"),
        check_vma=False,
    )
```

```python
import functools

import jax
import jax.numpy as jnp
import ml_dtypes
import numpy as np
from jax import lax
from jax.experimental import pallas as pl
from jax.experimental.pallas import tpu as pltpu
from jax.sharding import PartitionSpec as P

F = 4096
BAND = 128
MAXS = 4092
BINS = 64
LANES = 128
ROWS = 2 * F // LANES
BANDS = F // BAND
HEAD = (MAXS + 4) // LANES
VMEM_LIMIT = 48 * 1024 * 1024
MESH = pl.DeviceIdType.MESH


def tap_weights(frac_bin):
    offsets = jnp.arange(8, dtype=jnp.float32)
    spacing = offsets[None, :] - 3.0 - frac_bin.astype(jnp.float32)[:, None] / BINS
    return jnp.sinc(spacing) * jnp.sinc(spacing / 4.0)


def split_columns(matrix):
    high = matrix.astype(ml_dtypes.bfloat16)
    low = (matrix - high.astype(np.float64)).astype(ml_dtypes.bfloat16)
    return np.concatenate([high, high, low], axis=1)


def tables():
    r = np.arange(ROWS)
    lane = np.arange(LANES)
    band = np.arange(BANDS)
    first = 2 * np.pi * (np.outer(r, r) % ROWS) / ROWS
    first = split_columns(np.concatenate([np.cos(first), -np.sin(first)], axis=0))
    turn = 2 * np.pi * (np.outer(lane, lane) % (2 * F)) / (2 * F)
    twist = np.stack([np.cos(turn), np.sin(turn)]).astype(np.float32)
    second = 2 * np.pi * (np.outer(band, lane) % ROWS) / ROWS
    cos, sin = np.cos(second), np.sin(second)
    second = split_columns(np.block([[cos, sin], [-sin, cos]]))
    position = np.arange(2 * F).reshape(ROWS, LANES)
    hann = (0.5 - 0.5 * np.cos(2 * np.pi * position / (2 * F))).astype(np.float32)
    return first, twist, second, hann


def split_value(value):
    high = value.astype(jnp.bfloat16)
    low = (value - high.astype(jnp.float32)).astype(jnp.bfloat16)
    return high, low


def stack_kernel(
    shift_ref, taps_ref, raw_ref, first_ref, twist_ref, second_ref, hann_ref, out_ref,
    heading, following, tail, flat, white, recv, held,
    head_sems, send_sem, recv_sem, out_sem, in_sem,
):
    windows, owners, _, owned, nodes, _ = white.shape
    groups = recv.shape[0]
    scale = 1.0 / (owners * windows)
    step = 8
    together = 4
    me_w, me_g = lax.axis_index("win"), lax.axis_index("src")

    def wrap(index, count):
        return lax.rem(index + count, count)

    def start_heading():
        return pltpu.make_async_remote_copy(
            src_ref=heading,
            dst_ref=following,
            send_sem=head_sems.at[0],
            recv_sem=head_sems.at[1],
            device_id={"win": wrap(me_w - 1, owners)},
            device_id_type=MESH,
        )

    def across(w, d):
        target = wrap(me_w + d, owners)
        return pltpu.make_async_remote_copy(
            src_ref=white.at[w, target],
            dst_ref=recv.at[me_g, w, me_w],
            send_sem=send_sem.at[w, d],
            recv_sem=recv_sem.at[w, d],
            device_id={"win": target},
            device_id_type=MESH,
        )

    def arriving(w, d):
        return pltpu.make_async_remote_copy(
            src_ref=white.at[w, me_w],
            dst_ref=recv.at[me_g, w, wrap(me_w - d, owners)],
            send_sem=send_sem.at[w, d],
            recv_sem=recv_sem.at[w, d],
            device_id={"win": wrap(me_w + d, owners)},
            device_id_type=MESH,
        )

    def forward(w, e, d, group):
        place = recv.at[group, w, wrap(me_w - d, owners)]
        return pltpu.make_async_remote_copy(
            src_ref=place,
            dst_ref=place,
            send_sem=out_sem.at[w, e, d],
            recv_sem=in_sem.at[w, e, d],
            device_id={"src": wrap(me_g + e, groups)},
            device_id_type=MESH,
        )

    def pass_on(w, d):
        for e in range(1, groups):
            forward(w, e, d, me_g).start()
        slot = wrap(me_w - d, owners)
        re = recv[me_g, w, slot, 0].astype(jnp.float32) * scale
        im = recv[me_g, w, slot, 1].astype(jnp.float32) * scale
        held[0, w, slot] = re
        held[1, w, slot] = im
        held[2, w, slot] = re + im

    def serve(w, low, high):

        def body(d, carry):
            arriving(w, d).wait_recv()
            pass_on(w, d)
            return carry

        lax.fori_loop(low, high, body, 0)

    def spectra(w, samples, base):
        lane = lax.broadcasted_iota(jnp.int32, (ROWS, LANES), 1)

        def body(index, carry):
            columns = []
            for u in range(together):
                node = index * together + u
                total = jnp.zeros((ROWS, LANES), jnp.float32)
                for tap in range(8):
                    offset = jnp.maximum(shift_ref[node], 3) + (tap - 3)
                    row, by = offset // LANES, offset % LANES
                    here = samples[node, pl.ds(row + base, ROWS), :]
                    after = samples[node, pl.ds(row + base + 1, ROWS), :]
                    joined = jnp.where(lane >= by, here, after)
                    turned = pltpu.roll(joined, (LANES - by) % LANES, 1)
                    total = total + taps_ref[node, tap] * turned
                high, low = split_value(total * hann_ref[...])
                columns.append(jnp.concatenate([high, low, high], axis=0))
            section = jnp.dot(
                first_ref[...],
                jnp.concatenate(columns, axis=1),
                preferred_element_type=jnp.float32,
            )
            twisted = []
            for u in range(together):
                re = section[:ROWS, u * LANES : (u + 1) * LANES]
                im = section[ROWS:, u * LANES : (u + 1) * LANES]
                for half in range(2):
                    cos = twist_ref[0, half * ROWS : (half + 1) * ROWS, :]
                    sin = twist_ref[1, half * ROWS : (half + 1) * ROWS, :]
                    re_high, re_low = split_value(re * cos + im * sin)
                    im_high, im_low = split_value(im * cos - re * sin)
                    twisted.append(
                        jnp.concatenate(
                            [re_high, im_high, re_low, im_low, re_high, im_high], axis=1
                        )
                    )
            final = lax.dot_general(
                second_ref[...],
                jnp.concatenate(twisted, axis=0),
                (((1,), (1,)), ((), ())),
                preferred_element_type=jnp.float32,
            )
            for u in range(together):
                re = final[:BANDS, u * LANES : (u + 1) * LANES]
                im = final[BANDS:, u * LANES : (u + 1) * LANES]
                power = jnp.sum(re * re + im * im, axis=-1, keepdims=True) / BAND
                factor = lax.rsqrt(power + 1e-06)
                for part, value in ((0, re), (1, im)):
                    start = part * BANDS * nodes + index * together + u
                    flat[pl.ds(start, BANDS, stride=nodes), :] = value * factor
            return carry

        half = nodes // together // 2
        lax.fori_loop(0, half, body, 0)
        if w > 0:
            middle = (owners + 1) // 2
            serve(w - 1, 1, middle)
        lax.fori_loop(half, nodes // together, body, 0)
        if w > 0:
            serve(w - 1, middle, owners)
        for part in range(2):
            block = flat[part * BANDS * nodes : (part + 1) * BANDS * nodes, :]
            block = block.astype(jnp.bfloat16)
            white[w, :, part] = block.reshape(owners, owned, nodes, LANES)
        recv[me_g, w, me_w] = white[w, me_w]

    def send(w):

        def body(d, carry):
            across(w, d).start()
            return carry

        lax.fori_loop(1, owners, body, 0)
        pass_on(w, 0)

    def add(group, w):
        rows = pl.ds(pl.multiple_of(group * nodes, nodes), nodes)

        def band_body(band, carry):
            columns = pl.ds(pl.multiple_of(band * LANES, LANES), LANES)
            for chunk in range(nodes // step):

                def body(slot, sums):
                    sums = list(sums)
                    other_re = recv[group, w, slot, 0, band].astype(jnp.float32)
                    other_im = recv[group, w, slot, 1, band].astype(jnp.float32)
                    other_diff = other_re - other_im
                    for k in range(step):
                        i = chunk * step + k
                        sums[3 * k] += held[0, w, slot, band, i : i + 1, :] * other_re
                        sums[3 * k + 1] += held[1, w, slot, band, i : i + 1, :] * other_im
                        sums[3 * k + 2] += held[2, w, slot, band, i : i + 1, :] * other_diff
                    return tuple(sums)

                zero = jnp.zeros((nodes, LANES), jnp.float32)
                sums = lax.fori_loop(0, owners, body, (zero,) * (3 * step), unroll=4)
                for k in range(step):
                    p, q, r = sums[3 * k : 3 * k + 3]
                    i = chunk * step + k
                    if w == 0:
                        out_ref[0, i, rows, columns] = p + q
                        out_ref[1, i, rows, columns] = r - p + q
                    else:
                        out_ref[0, i, rows, columns] += p + q
                        out_ref[1, i, rows, columns] += r - p + q
            return carry

        lax.fori_loop(0, owned, band_body, 0)

    def finish(w):

        def body(e, carry):
            group = wrap(me_g - e, groups)

            def landed(d, inner):
                forward(w, e, d, group).wait_recv()
                return inner

            lax.fori_loop(0, owners, landed, 0)
            add(group, w)
            return carry

        lax.fori_loop(1, groups, body, 0)

    barrier = pltpu.get_barrier_semaphore()
    for d in range(1, owners):
        pl.semaphore_signal(
            barrier, inc=1, device_id={"win": wrap(me_w + d, owners)}, device_id_type=MESH
        )
    for e in range(1, groups):
        pl.semaphore_signal(
            barrier, inc=1, device_id={"src": wrap(me_g + e, groups)}, device_id_type=MESH
        )
    heading[...] = raw_ref[:, :HEAD, :].astype(jnp.bfloat16)

    for w in range(windows):
        if w < windows - 1:
            spectra(w, raw_ref, w * ROWS)
        else:
            @pl.when(me_w < owners - 1)
            def _():
                start_heading().wait_recv()

            @pl.when(me_w == owners - 1)
            def _():
                following[...] = jnp.zeros_like(following)

            tail[:, :ROWS, :] = raw_ref[:, w * ROWS :, :]
            tail[:, ROWS : ROWS + HEAD, :] = following[...].astype(jnp.float32)
            tail[:, ROWS + HEAD :, :] = jnp.zeros((nodes, 8, LANES), jnp.float32)
            spectra(w, tail, 0)
        if w == 0:
            pl.semaphore_wait(barrier, owners + groups - 2)

            @pl.when(me_w > 0)
            def _():
                start_heading().start()

        send(w)
        if w >= 1:
            add(me_g, w - 1)
        if w >= 2:
            finish(w - 2)
    serve(windows - 1, 1, owners)
    if windows >= 2:
        finish(windows - 2)
    add(me_g, windows - 1)
    finish(windows - 1)

    @pl.when(me_w > 0)
    def _():
        start_heading().wait_send()

    for w in range(windows):

        def sent(d, carry):
            across(w, d).wait_send()
            return carry

        lax.fori_loop(1, owners, sent, 0)

        def passed(d, carry):
            for e in range(1, groups):
                forward(w, e, d, me_g).wait_send()
            return carry

        lax.fori_loop(0, owners, passed, 0)


def stacked(raw, shift, taps, owners, groups):
    nodes, rows = raw.shape[:2]
    windows = rows // ROWS
    owned = BANDS // owners
    chunk = (2, owned, nodes, LANES)
    constants = [jnp.asarray(table) for table in tables()]
    smem = pl.BlockSpec(memory_space=pltpu.SMEM)
    vmem = pl.BlockSpec(memory_space=pltpu.VMEM)
    return pl.pallas_call(
        stack_kernel,
        out_shape=jax.ShapeDtypeStruct((2, nodes, groups * nodes, owned * LANES), jnp.float32),
        in_specs=[smem, smem] + [vmem] * 5,
        out_specs=vmem,
        scratch_shapes=[
            pltpu.VMEM((nodes, HEAD, LANES), jnp.bfloat16),
            pltpu.VMEM((nodes, HEAD, LANES), jnp.bfloat16),
            pltpu.VMEM((nodes, ROWS + HEAD + 8, LANES), jnp.float32),
            pltpu.VMEM((2 * BANDS * nodes, LANES), jnp.float32),
            pltpu.VMEM((windows, owners) + chunk, jnp.bfloat16),
            pltpu.VMEM((groups, windows, owners) + chunk, jnp.bfloat16),
            pltpu.VMEM((3, windows, owners) + chunk[1:], jnp.float32),
            pltpu.SemaphoreType.DMA((2,)),
            pltpu.SemaphoreType.DMA((windows, owners)),
            pltpu.SemaphoreType.DMA((windows, owners)),
            pltpu.SemaphoreType.DMA((windows, groups, owners)),
            pltpu.SemaphoreType.DMA((windows, groups, owners)),
        ],
        compiler_params=pltpu.CompilerParams(
            collective_id=0, has_side_effects=True, vmem_limit_bytes=VMEM_LIMIT
        ),
    )(shift, taps, raw, *constants)


def local(raw, shift, frac_bin):
    owners = lax.axis_size("win")
    raw = raw.reshape(raw.shape[0], -1, LANES)
    return stacked(raw, shift, tap_weights(frac_bin), owners, lax.axis_size("src"))


def solution(mesh):
    return jax.shard_map(
        local,
        mesh=mesh,
        in_specs=(P("src", "win"), P("src"), P("src")),
        out_specs=P(None, "src", None, "win"),
        check_vma=False,
    )
```

```python
import functools

import jax
import jax.numpy as jnp
import ml_dtypes
import numpy as np
from jax import lax
from jax.experimental import pallas as pl
from jax.experimental.pallas import tpu as pltpu
from jax.sharding import PartitionSpec as P

F = 4096
BAND = 128
MAXS = 4092
BINS = 64
LANES = 128
ROWS = 2 * F // LANES
BANDS = F // BAND
HEAD = (MAXS + 4) // LANES
VMEM_LIMIT = 32 * 1024 * 1024
MESH = pl.DeviceIdType.MESH


def tap_weights(frac_bin):
    offsets = jnp.arange(8, dtype=jnp.float32)
    spacing = offsets[None, :] - 3.0 - frac_bin.astype(jnp.float32)[:, None] / BINS
    return jnp.sinc(spacing) * jnp.sinc(spacing / 4.0)


def split_columns(matrix):
    high = matrix.astype(ml_dtypes.bfloat16)
    low = (matrix - high.astype(np.float64)).astype(ml_dtypes.bfloat16)
    return np.concatenate([high, high, low], axis=1)


def tables():
    r = np.arange(ROWS)
    lane = np.arange(LANES)
    band = np.arange(BANDS)
    first = 2 * np.pi * (np.outer(r, r) % ROWS) / ROWS
    first = split_columns(np.concatenate([np.cos(first), -np.sin(first)], axis=0))
    turn = 2 * np.pi * (np.outer(lane, lane) % (2 * F)) / (2 * F)
    twist = np.stack([np.cos(turn), np.sin(turn)]).astype(np.float32)
    second = 2 * np.pi * (np.outer(band, lane) % ROWS) / ROWS
    cos, sin = np.cos(second), np.sin(second)
    second = split_columns(np.block([[cos, sin], [-sin, cos]]))
    position = np.arange(2 * F).reshape(ROWS, LANES)
    hann = (0.5 - 0.5 * np.cos(2 * np.pi * position / (2 * F))).astype(np.float32)
    return first, twist, second, hann


def split_value(value):
    high = value.astype(jnp.bfloat16)
    low = (value - high.astype(jnp.float32)).astype(jnp.bfloat16)
    return high, low


def stack_kernel(
    shift_ref, taps_ref, raw_ref, first_ref, twist_ref, second_ref, hann_ref, out_ref,
    heading, following, tail, flat, white, recv, held,
    head_sems, send_sem, recv_sem, out_sem, in_sem,
):
    windows, owners, _, owned, nodes, _ = white.shape
    groups = recv.shape[0]
    scale = 1.0 / (owners * windows)
    step = 8
    together = 4
    me_w, me_g = lax.axis_index("win"), lax.axis_index("src")

    def wrap(index, count):
        return lax.rem(index + count, count)

    def start_heading():
        return pltpu.make_async_remote_copy(
            src_ref=heading,
            dst_ref=following,
            send_sem=head_sems.at[0],
            recv_sem=head_sems.at[1],
            device_id={"win": wrap(me_w - 1, owners)},
            device_id_type=MESH,
        )

    def across(w, d):
        target = wrap(me_w + d, owners)
        return pltpu.make_async_remote_copy(
            src_ref=white.at[w, target],
            dst_ref=recv.at[me_g, w, me_w],
            send_sem=send_sem.at[w, d],
            recv_sem=recv_sem.at[w, d],
            device_id={"win": target},
            device_id_type=MESH,
        )

    def arriving(w, d):
        return pltpu.make_async_remote_copy(
            src_ref=white.at[w, me_w],
            dst_ref=recv.at[me_g, w, wrap(me_w - d, owners)],
            send_sem=send_sem.at[w, d],
            recv_sem=recv_sem.at[w, d],
            device_id={"win": wrap(me_w + d, owners)},
            device_id_type=MESH,
        )

    square = groups == 4
    beside = me_g + 1 - 2 * lax.rem(me_g, 2)
    above = lax.rem(me_g + 2, 4)
    corner = 3 - me_g

    def target_of(e):
        return wrap(me_g + e, groups) if not square else (beside if e == 1 else above)

    def relay(w, e, d, group, part):
        place = recv.at[group, w, wrap(me_w - d, owners), part]
        return pltpu.make_async_remote_copy(
            src_ref=place,
            dst_ref=place,
            send_sem=out_sem.at[w, e, d],
            recv_sem=in_sem.at[w, e, d],
            device_id={"src": above if part == 0 else beside},
            device_id_type=MESH,
        )

    def forward(w, e, d, group):
        place = recv.at[group, w, wrap(me_w - d, owners)]
        return pltpu.make_async_remote_copy(
            src_ref=place,
            dst_ref=place,
            send_sem=out_sem.at[w, e, d],
            recv_sem=in_sem.at[w, e, d],
            device_id={"src": target_of(e)},
            device_id_type=MESH,
        )

    direct = range(1, 3) if square else range(1, groups)

    def pass_on(w, d):
        for e in direct:
            forward(w, e, d, me_g).start()
        slot = wrap(me_w - d, owners)
        re = recv[me_g, w, slot, 0].astype(jnp.float32) * scale
        im = recv[me_g, w, slot, 1].astype(jnp.float32) * scale
        held[0, w, slot] = re
        held[1, w, slot] = im
        held[2, w, slot] = re + im

    def serve(w, low, high):

        def body(d, carry):
            arriving(w, d).wait_recv()
            pass_on(w, d)
            return carry

        lax.fori_loop(low, high, body, 0)

    def spectra(w, samples, base):
        lane = lax.broadcasted_iota(jnp.int32, (ROWS, LANES), 1)

        def body(index, carry):
            columns = []
            for u in range(together):
                node = index * together + u
                total = jnp.zeros((ROWS, LANES), jnp.float32)
                for tap in range(8):
                    offset = jnp.maximum(shift_ref[node], 3) + (tap - 3)
                    row, by = offset // LANES, offset % LANES
                    here = samples[node, pl.ds(row + base, ROWS), :]
                    after = samples[node, pl.ds(row + base + 1, ROWS), :]
                    joined = jnp.where(lane >= by, here, after)
                    turned = pltpu.roll(joined, (LANES - by) % LANES, 1)
                    total = total + taps_ref[node, tap] * turned
                high, low = split_value(total * hann_ref[...])
                columns.append(jnp.concatenate([high, low, high], axis=0))
            section = jnp.dot(
                first_ref[...],
                jnp.concatenate(columns, axis=1),
                preferred_element_type=jnp.float32,
            )
            twisted = []
            for u in range(together):
                re = section[:ROWS, u * LANES : (u + 1) * LANES]
                im = section[ROWS:, u * LANES : (u + 1) * LANES]
                for half in range(2):
                    cos = twist_ref[0, half * ROWS : (half + 1) * ROWS, :]
                    sin = twist_ref[1, half * ROWS : (half + 1) * ROWS, :]
                    re_high, re_low = split_value(re * cos + im * sin)
                    im_high, im_low = split_value(im * cos - re * sin)
                    twisted.append(
                        jnp.concatenate(
                            [re_high, im_high, re_low, im_low, re_high, im_high], axis=1
                        )
                    )
            final = lax.dot_general(
                second_ref[...],
                jnp.concatenate(twisted, axis=0),
                (((1,), (1,)), ((), ())),
                preferred_element_type=jnp.float32,
            )
            for u in range(together):
                re = final[:BANDS, u * LANES : (u + 1) * LANES]
                im = final[BANDS:, u * LANES : (u + 1) * LANES]
                power = jnp.sum(re * re + im * im, axis=-1, keepdims=True) / BAND
                factor = lax.rsqrt(power + 1e-06)
                for part, value in ((0, re), (1, im)):
                    start = part * BANDS * nodes + index * together + u
                    flat[pl.ds(start, BANDS, stride=nodes), :] = value * factor
            return carry

        half = nodes // together // 2
        lax.fori_loop(0, half, body, 0)
        if w > 0:
            middle = (owners + 1) // 2
            serve(w - 1, 1, middle)
        lax.fori_loop(half, nodes // together, body, 0)
        if w > 0:
            serve(w - 1, middle, owners)
        for part in range(2):
            block = flat[part * BANDS * nodes : (part + 1) * BANDS * nodes, :]
            block = block.astype(jnp.bfloat16)
            white[w, :, part] = block.reshape(owners, owned, nodes, LANES)
        recv[me_g, w, me_w] = white[w, me_w]

    def send(w):

        def body(d, carry):
            across(w, d).start()
            return carry

        lax.fori_loop(1, owners, body, 0)
        pass_on(w, 0)

    def add(group, w):
        rows = pl.ds(pl.multiple_of(group * nodes, nodes), nodes)

        def band_body(band, carry):
            columns = pl.ds(pl.multiple_of(band * LANES, LANES), LANES)
            for chunk in range(nodes // step):

                def body(slot, sums):
                    sums = list(sums)
                    other_re = recv[group, w, slot, 0, band].astype(jnp.float32)
                    other_im = recv[group, w, slot, 1, band].astype(jnp.float32)
                    other_diff = other_re - other_im
                    for k in range(step):
                        i = chunk * step + k
                        sums[3 * k] += held[0, w, slot, band, i : i + 1, :] * other_re
                        sums[3 * k + 1] += held[1, w, slot, band, i : i + 1, :] * other_im
                        sums[3 * k + 2] += held[2, w, slot, band, i : i + 1, :] * other_diff
                    return tuple(sums)

                zero = jnp.zeros((nodes, LANES), jnp.float32)
                sums = lax.fori_loop(0, owners, body, (zero,) * (3 * step), unroll=4)
                for k in range(step):
                    p, q, r = sums[3 * k : 3 * k + 3]
                    i = chunk * step + k
                    if w == 0:
                        out_ref[0, i, rows, columns] = p + q
                        out_ref[1, i, rows, columns] = r - p + q
                    else:
                        out_ref[0, i, rows, columns] += p + q
                        out_ref[1, i, rows, columns] += r - p + q
            return carry

        lax.fori_loop(0, owned, band_body, 0)

    def finish_corner(w):

        def landed(d, carry):
            relay(w, 3, d, corner, 0).wait_recv()
            relay(w, 0, d, corner, 1).wait_recv()
            return carry

        lax.fori_loop(0, owners, landed, 0)
        add(corner, w)

    def finish(w):
        if square:

            def landed(d, carry):
                forward(w, 1, d, beside).wait_recv()
                relay(w, 3, d, beside, 0).start()
                forward(w, 2, d, above).wait_recv()
                relay(w, 0, d, above, 1).start()
                return carry

            lax.fori_loop(0, owners, landed, 0)
            if w >= 1:
                finish_corner(w - 1)
            add(beside, w)
            add(above, w)
            return

        def body(e, carry):
            group = wrap(me_g - e, groups)

            def landed(d, inner):
                forward(w, e, d, group).wait_recv()
                return inner

            lax.fori_loop(0, owners, landed, 0)
            add(group, w)
            return carry

        lax.fori_loop(1, groups, body, 0)

    barrier = pltpu.get_barrier_semaphore()
    for d in range(1, owners):
        pl.semaphore_signal(
            barrier, inc=1, device_id={"win": wrap(me_w + d, owners)}, device_id_type=MESH
        )
    for e in range(1, groups):
        pl.semaphore_signal(
            barrier, inc=1, device_id={"src": wrap(me_g + e, groups)}, device_id_type=MESH
        )
    heading[...] = raw_ref[:, :HEAD, :].astype(jnp.bfloat16)

    for w in range(windows):
        if w < windows - 1:
            spectra(w, raw_ref, w * ROWS)
        else:
            @pl.when(me_w < owners - 1)
            def _():
                start_heading().wait_recv()

            @pl.when(me_w == owners - 1)
            def _():
                following[...] = jnp.zeros_like(following)

            tail[:, :ROWS, :] = raw_ref[:, w * ROWS :, :]
            tail[:, ROWS : ROWS + HEAD, :] = following[...].astype(jnp.float32)
            tail[:, ROWS + HEAD :, :] = jnp.zeros((nodes, 8, LANES), jnp.float32)
            spectra(w, tail, 0)
        if w == 0:
            pl.semaphore_wait(barrier, owners + groups - 2)

            @pl.when(me_w > 0)
            def _():
                start_heading().start()

        send(w)
        if w >= 1:
            add(me_g, w - 1)
        if w >= 2:
            finish(w - 2)
    serve(windows - 1, 1, owners)
    if windows >= 2:
        finish(windows - 2)
    add(me_g, windows - 1)
    finish(windows - 1)
    if square:
        finish_corner(windows - 1)

    @pl.when(me_w > 0)
    def _():
        start_heading().wait_send()

    for w in range(windows):

        def sent(d, carry):
            across(w, d).wait_send()
            return carry

        lax.fori_loop(1, owners, sent, 0)

        def passed(d, carry):
            for e in direct:
                forward(w, e, d, me_g).wait_send()
            if square:
                relay(w, 3, d, beside, 0).wait_send()
                relay(w, 0, d, above, 1).wait_send()
            return carry

        lax.fori_loop(0, owners, passed, 0)


def stacked(raw, shift, taps, owners, groups):
    nodes, rows = raw.shape[:2]
    windows = rows // ROWS
    owned = BANDS // owners
    chunk = (2, owned, nodes, LANES)
    constants = [jnp.asarray(table) for table in tables()]
    smem = pl.BlockSpec(memory_space=pltpu.SMEM)
    vmem = pl.BlockSpec(memory_space=pltpu.VMEM)
    return pl.pallas_call(
        stack_kernel,
        out_shape=jax.ShapeDtypeStruct((2, nodes, groups * nodes, owned * LANES), jnp.float32),
        in_specs=[smem, smem] + [vmem] * 5,
        out_specs=vmem,
        scratch_shapes=[
            pltpu.VMEM((nodes, HEAD, LANES), jnp.bfloat16),
            pltpu.VMEM((nodes, HEAD, LANES), jnp.bfloat16),
            pltpu.VMEM((nodes, ROWS + HEAD + 8, LANES), jnp.float32),
            pltpu.VMEM((2 * BANDS * nodes, LANES), jnp.float32),
            pltpu.VMEM((windows, owners) + chunk, jnp.bfloat16),
            pltpu.VMEM((groups, windows, owners) + chunk, jnp.bfloat16),
            pltpu.VMEM((3, windows, owners) + chunk[1:], jnp.float32),
            pltpu.SemaphoreType.DMA((2,)),
            pltpu.SemaphoreType.DMA((windows, owners)),
            pltpu.SemaphoreType.DMA((windows, owners)),
            pltpu.SemaphoreType.DMA((windows, groups, owners)),
            pltpu.SemaphoreType.DMA((windows, groups, owners)),
        ],
        compiler_params=pltpu.CompilerParams(
            collective_id=0, has_side_effects=True, vmem_limit_bytes=VMEM_LIMIT
        ),
    )(shift, taps, raw, *constants)


def local(raw, shift, frac_bin):
    owners = lax.axis_size("win")
    raw = raw.reshape(raw.shape[0], -1, LANES)
    return stacked(raw, shift, tap_weights(frac_bin), owners, lax.axis_size("src"))


def solution(mesh):
    return jax.shard_map(
        local,
        mesh=mesh,
        in_specs=(P("src", "win"), P("src"), P("src")),
        out_specs=P(None, "src", None, "win"),
        check_vma=False,
    )
```
